32 devices in a mesh: ep: 16 (over z, y, x), dp: 2 (over core).
Axes of the slice: x: 2, y: 2, z: 4, core: 2. Of those that a mesh axis runs over, the one named last changes fastest.
Arguments:
- tokens: bfloat16 [4096, 768], P(('ep', 'dp')), may hold values from -6 to 6
- routing: int32 [4096, 1], P(('ep', 'dp')), may hold values from 0 to 15; in each aligned block of 128 rows (0 to 127, 128 to 255, ...) at most 16 rows name the same one
- gate_prob: float32 [4096], P(('ep', 'dp')), may hold values from 0.2 to 1
- up_weight: bfloat16 [16, 768, 3072], P('ep', None, 'dp'), may hold values from -0.21875 to 0.21875
- down_weight: bfloat16 [16, 3072, 768], P('ep', 'dp'), may hold values from -0.109375 to 0.109375
- out_grad: bfloat16 [4096, 768], P(('ep', 'dp')), may hold values from -1.5 to 1.5
Outputs:
- output: bfloat16 [4096, 768], P(('ep', 'dp'))
- token_grad: bfloat16 [4096, 768], P(('ep', 'dp'))
- prob_grad: float32 [4096], P(('ep', 'dp'))
- up_grad: bfloat16 [16, 768, 3072], P('ep', None, 'dp')
- down_grad: bfloat16 [16, 3072, 768], P('ep', 'dp')
The draws below stay inside these ranges and needn't reach their ends.
Inputs may be any that keep to these rules, and one draw needn't show every extreme that they name: `routing`: among the 128 rows of one device (devices in the order of ep, then dp) no expert is named more than 16 times; in some devices' rows some expert is named exactly 16 times; every expert is named somewhere.
All inputs are finite; a program needn't handle non-finite values.
Results may differ from the reference program's by a relative error of at most 0.0058.
Values may be sent and summed in bfloat16 or wider, within the bound.
A program may use at most 64 MiB of HBM per device.

```python
import math
import jax
import jax.numpy as jnp
import numpy as np
from jax import lax

D = 768
FF = 3072
TOK_DEV = 128
EXPERTS = 16
CAP = 16
TOKENS = 4096
N_EP = 16
N_DP = 2


def levels(rng, extent, split, least, top_value):
    gain = 1.0
    for position, parts in split:
        heights = jax.random.uniform(jax.random.fold_in(jax.random.fold_in(rng, 6), position), (parts,), jnp.float32, least / len(split), top_value / len(split))
        gain = gain * jnp.repeat(jnp.exp(heights), extent[position] // parts).reshape((-1,) + (1,) * (len(extent) - 1 - position))
    return gain


def shared_out(own_key, own, number, rows, count, top, reach, lean):
    order = jax.random.permutation(own_key, count)
    crowded, ordinary = portions_of(count, rows * top, reach, lean, True), portions_of(count, rows * top, reach, lean, False)
    places = jnp.arange(count)

    def named(sizes, turn):
        used = int((sizes > 0).sum())
        fixed = max(1, used // 4)
        moved = fixed + (places - fixed + turn * (used - fixed)) % max(1, count - fixed)
        return jnp.zeros((count,), jnp.int32).at[order[jnp.where(places < fixed, places, moved)]].set(jnp.asarray(sizes, jnp.int32))

    sizes = jnp.where(number % 4 == 0, named(crowded, number // 4), named(ordinary, number - number // 4 - 1))
    mixed = jax.random.permutation(jax.random.fold_in(own, 3), count)
    source_of, receiver = mixed[0:count // 2 * 2:2], mixed[1:count // 2 * 2:2]
    room = jnp.minimum(sizes[source_of] - 1, reach - sizes[receiver]) // 2
    room = jnp.where((source_of == order[0]) | (receiver == order[0]) | (sizes[receiver] == 0), 0, jnp.maximum(room, 0))
    moved = jax.random.randint(jax.random.fold_in(own, 4), (count // 2,), 0, 1 << 20) % (room + 1)
    sizes = sizes.at[source_of].add(-moved).at[receiver].add(moved)
    members = jnp.searchsorted(jnp.cumsum(sizes), jnp.arange(rows * top), side="right").astype(jnp.int32)
    listing = members.reshape(top, rows).T
    listing = listing[jax.random.permutation(jax.random.fold_in(own, 1), rows)]
    turn = jax.random.randint(jax.random.fold_in(own, 2), (rows, 1), 0, top)
    return jnp.take_along_axis(listing, (jnp.arange(top)[None, :] + turn) % top, axis=1)


def portions_of(number_of, total, limit, slope, full):
    portions = [(1 << 20) // math.isqrt(standing ** slope) + 1 for standing in range(1, number_of + 1)]
    largest = limit if full else min(limit, max(-(-total // number_of), total * portions[0] // sum(portions)))
    least = 1 if total - largest >= number_of - 1 else 0
    holding, rest = [largest] + [least] * (number_of - 1), total - largest - least * (number_of - 1)
    while rest > 0:
        movable = [i for i in range(1, number_of) if holding[i] < largest] or [i for i in range(1, number_of) if holding[i] < limit]
        pool, budget = sum([portions[i] for i in movable]), rest
        for i in movable:
            addition = min(limit - holding[i], max(1, budget * portions[i] // pool), rest)
            holding[i] = holding[i] + addition
            rest = rest - addition
    return np.array(holding)


def normal_values(rng, shape, width, limit, pieces=(), kind=jnp.bfloat16):
    loudness = levels(rng, shape, pieces, -0.22, 0.18) if pieces else 1.0
    entries = jax.random.normal(rng, shape, jnp.float32) * width * loudness
    return jnp.minimum(jnp.maximum(entries, -limit), limit).astype(kind)


def setup_inputs(seed: int = 0) -> dict:
    keys = jax.random.split(jax.random.key(seed), 7)
    tokens = normal_values(keys[0], (TOKENS, D), 1.0, 6.0, ((0, 32),))
    routing_keys = jax.random.split(jax.random.fold_in(keys[1], 1), TOKENS // TOK_DEV)
    routing_turns = jax.random.permutation(jax.random.fold_in(keys[1], 3), TOKENS // TOK_DEV)
    routing = jax.vmap(lambda own, number: shared_out(jax.random.fold_in(keys[1], 2), own, number, TOK_DEV, EXPERTS, 1, CAP, 1))(routing_keys, routing_turns).reshape((TOKENS, 1))
    gate_prob = jnp.clip(0.2 + 0.8 * jax.random.uniform(keys[2], (TOKENS,), jnp.float32) ** levels(keys[2], (TOKENS,), ((0, 32),), -0.2, 0.2), 0.2, 1.0)
    up_weight = normal_values(keys[3], (EXPERTS, D, FF), D ** -0.5, 0.21875, ((0, 16), (2, 2)))
    down_weight = normal_values(keys[4], (EXPERTS, FF, D), FF ** -0.5, 0.109375, ((0, 16), (1, 2)))
    out_grad = normal_values(keys[5], (TOKENS, D), 0.25, 1.5, ((0, 32),))
    return dict(tokens=tokens, routing=routing, gate_prob=gate_prob, up_weight=up_weight, down_weight=down_weight, out_grad=out_grad)


def one_expert(packed):
    rows_in, up_mat, down_mat, grad_in = packed
    up_full = up_mat.astype(jnp.float32)
    down_full = down_mat.astype(jnp.float32)
    preact = jnp.dot(rows_in.astype(jnp.float32), up_full)
    activated, back_fn = jax.vjp(jax.nn.gelu, preact)
    hidden = activated.astype(jnp.bfloat16)
    hidden_wide = hidden.astype(jnp.float32)
    result_rows = jnp.dot(hidden_wide, down_full).astype(jnp.bfloat16)
    grad_wide = grad_in.astype(jnp.float32)
    hidden_grad = jnp.dot(grad_wide, down_full.T)
    preact_grad = back_fn(hidden_grad)[0].astype(jnp.bfloat16)
    preact_wide = preact_grad.astype(jnp.float32)
    input_rows = jnp.dot(preact_wide, up_full.T).astype(jnp.bfloat16)
    up_sum = jnp.dot(rows_in.astype(jnp.float32).T, preact_wide).astype(jnp.bfloat16)
    down_sum = jnp.dot(hidden_wide.T, grad_wide).astype(jnp.bfloat16)
    return (result_rows, input_rows, up_sum, down_sum)

def reference(tokens, routing, gate_prob, up_weight, down_weight, out_grad):
    sources = N_EP * N_DP
    expert = routing[:, 0].astype(jnp.int32)
    onehot = (expert[:, None] == jnp.arange(EXPERTS, dtype=jnp.int32)[None, :]).astype(jnp.int32)
    blocks = onehot.reshape(sources, TOK_DEV, EXPERTS)
    ranking = lax.optimization_barrier(jnp.sum((jnp.cumsum(blocks, axis=1) - blocks) * blocks, axis=2)).reshape(-1)
    source = jnp.arange(TOKENS, dtype=jnp.int32) // TOK_DEV
    column = (source * CAP + ranking).astype(jnp.int32)
    empty = jnp.zeros((EXPERTS, sources * CAP, D), jnp.bfloat16)
    rows_all = empty.at[expert, column].set(tokens)
    scaled = (gate_prob[:, None] * out_grad.astype(jnp.float32)).astype(jnp.bfloat16)
    grads_all = empty.at[expert, column].set(scaled)
    results, inputs, up_grad, down_grad = lax.map(one_expert, (rows_all, up_weight, down_weight, grads_all))
    expert_out = results[expert, column].astype(jnp.float32)
    output = (gate_prob[:, None] * expert_out).astype(jnp.bfloat16)
    prob_grad = lax.optimization_barrier(jnp.sum(out_grad.astype(jnp.float32) * expert_out, axis=1))
    token_grad = inputs[expert, column]
    return (output, token_grad, prob_grad, up_grad, down_grad)
```

```python
import functools

import jax
import jax.numpy as jnp
from jax import lax
from jax.experimental import pallas as pl
from jax.experimental.pallas import tpu as pltpu
from jax.sharding import PartitionSpec as P


def local_plain(tokens, routing, gate_prob, up_weight, down_weight, out_grad):
    token_count = tokens.shape[0]
    local_experts = up_weight.shape[0]
    peer_count = lax.axis_size("ep")
    experts = local_experts * peer_count
    capacity = max(2, 2 * token_count // experts)
    slot_count = experts * capacity
    expert = routing[:, 0]
    onehot = (expert[:, None] == jnp.arange(experts, dtype=jnp.int32)[None, :]).astype(jnp.int32)
    ranking = jnp.sum((jnp.cumsum(onehot, axis=0) - onehot) * onehot, axis=1)
    target = expert * capacity + ranking
    placing = (jnp.arange(slot_count, dtype=jnp.int32)[:, None] == target[None, :]).astype(
        jnp.bfloat16
    )

    def dispatch(values):
        packed = jnp.dot(placing, values, preferred_element_type=jnp.float32).astype(jnp.bfloat16)
        return packed.reshape(experts, capacity, values.shape[1])

    def collect(returned):
        flat = returned.reshape(slot_count, returned.shape[2])
        return jnp.einsum("st,sd->td", placing, flat, preferred_element_type=jnp.float32)

    grad_wide = out_grad.astype(jnp.float32)
    scaled = (gate_prob[:, None] * grad_wide).astype(jnp.bfloat16)
    sent_rows = lax.all_to_all(dispatch(tokens), "ep", split_axis=0, concat_axis=1, tiled=True)
    expert_rows = lax.all_gather(sent_rows, "dp", axis=1, tiled=True)
    up_full, down_full = (up_weight, down_weight)
    preact = jnp.einsum("erd,edf->erf", expert_rows, up_full, preferred_element_type=jnp.float32)
    activated, back_fn = jax.vjp(jax.nn.gelu, preact)
    hidden = activated.astype(jnp.bfloat16)
    partial_out = jnp.einsum("erf,efd->erd", hidden, down_full, preferred_element_type=jnp.float32)
    merged = lax.psum_scatter(partial_out, "dp", scatter_dimension=1, tiled=True)
    expert_out = lax.all_to_all(
        merged.astype(jnp.bfloat16), "ep", split_axis=1, concat_axis=0, tiled=True
    )
    expert_tok = collect(expert_out)
    output = (gate_prob[:, None] * expert_tok).astype(jnp.bfloat16)
    prob_grad = jnp.sum(grad_wide * expert_tok, axis=1)
    sent_grads = lax.all_to_all(dispatch(scaled), "ep", split_axis=0, concat_axis=1, tiled=True)
    grad_rows = lax.all_gather(sent_grads, "dp", axis=1, tiled=True)
    hidden_grad = jnp.einsum(
        "erd,efd->erf", grad_rows, down_full, preferred_element_type=jnp.float32
    )
    preact_grad = back_fn(hidden_grad)[0].astype(jnp.bfloat16)
    partial_input = jnp.einsum(
        "erf,edf->erd", preact_grad, up_full, preferred_element_type=jnp.float32
    )
    up_sum = jnp.einsum(
        "erd,erf->edf", expert_rows, preact_grad, preferred_element_type=jnp.float32
    )
    down_sum = jnp.einsum("erf,erd->efd", hidden, grad_rows, preferred_element_type=jnp.float32)
    input_rows = lax.psum_scatter(partial_input, "dp", scatter_dimension=1, tiled=True)
    up_grad = up_sum.astype(jnp.bfloat16)
    down_grad = down_sum.astype(jnp.bfloat16)
    returned = lax.all_to_all(
        input_rows.astype(jnp.bfloat16), "ep", split_axis=1, concat_axis=0, tiled=True
    )
    token_grad = collect(returned).astype(jnp.bfloat16)
    return (output, token_grad, prob_grad, up_grad, down_grad)


MESH = pl.DeviceIdType.MESH
TILE = 16
CHUNK = 256
SCALE = 0.7978845608028654
CUBIC = 0.044715


def row_block(start, size):
    return pl.ds(pl.multiple_of(start, TILE), size)


def kernel(
    n,
    cap,
    tok_ref,
    route_ref,
    gate_ref,
    up_hbm,
    down_hbm,
    grad_ref,
    out_ref,
    tgrad_ref,
    pgrad_ref,
    ugrad_ref,
    dgrad_ref,
    up,
    down,
    tok_send,
    grad_send,
    rows,
    grads,
    rows_t,
    hidden,
    slope,
    dpre,
    mine,
    merge_send,
    merge_recv,
    ret_send,
    ret_recv,
    placing_t,
    weight_sem,
    ep_send,
    ep_recv,
    dp_send,
    dp_recv,
    merge_ssem,
    merge_rsem,
):
    me, core = lax.axis_index("ep"), lax.axis_index("dp")
    partner = (me, 1 - core)
    slots = n * cap
    count, width = tok_ref.shape
    units = up.shape[1]

    barrier = pltpu.get_barrier_semaphore()

    @pl.loop(1, n)
    def _(k):
        pl.semaphore_signal(
            barrier, inc=1, device_id=(lax.rem(me + k, n), core), device_id_type=MESH
        )

    pl.semaphore_signal(barrier, inc=1, device_id=partner, device_id_type=MESH)
    up_copy = pltpu.make_async_copy(up_hbm.at[0], up, weight_sem.at[0])
    down_copy = pltpu.make_async_copy(down_hbm.at[0], down, weight_sem.at[1])
    up_copy.start()
    down_copy.start()

    def remote(src, dst, ssem, rsem, device):
        return pltpu.make_async_remote_copy(
            src_ref=src,
            dst_ref=dst,
            send_sem=ssem,
            recv_sem=rsem,
            device_id=device,
            device_id_type=MESH,
        )

    def exchange(kind, src, dst, peer, slot):
        return remote(
            src.at[row_block(peer * cap, cap)],
            dst.at[row_block(slot * cap, cap)],
            ep_send.at[kind, peer],
            ep_recv.at[kind, slot],
            (peer, core),
        )

    def send_all(kind, src, dst):
        @pl.loop(1, n)
        def _(k):
            exchange(kind, src, dst, lax.rem(me + k, n), me).start()

        dst[row_block(me * cap, cap), :] = src[row_block(me * cap, cap), :]

    def wait_block(kind, src, dst, source):
        exchange(kind, src, dst, source, source).wait_recv()

    def forward(kind, buf, source):
        return remote(
            buf.at[row_block(source * cap, cap)],
            buf.at[row_block(slots + source * cap, cap)],
            dp_send.at[kind, source],
            dp_recv.at[kind, source],
            partner,
        )

    def share(kind, src, dst):
        forward(kind, dst, me).start()

        @pl.loop(1, n)
        def _(k):
            source = lax.rem(me + k, n)
            wait_block(kind, src, dst, source)
            forward(kind, dst, source).start()

        @pl.loop(0, n)
        def _(k):
            forward(kind, dst, k).wait_recv()

    eye = lax.broadcasted_iota(jnp.int32, (count, count), 0) == lax.broadcasted_iota(
        jnp.int32, (count, count), 1
    )

    def to_column(row):
        return jnp.sum(jnp.where(eye, row, 0.0), axis=1, keepdims=True)

    expert = route_ref[...]
    onehot = (lax.broadcasted_iota(jnp.int32, (n, count), 0) == expert).astype(jnp.float32)
    before = (
        lax.broadcasted_iota(jnp.int32, (count, count), 0)
        < lax.broadcasted_iota(jnp.int32, (count, count), 1)
    ).astype(jnp.float32)
    earlier = jnp.dot(
        onehot.astype(jnp.bfloat16),
        before.astype(jnp.bfloat16),
        preferred_element_type=jnp.float32,
    )
    target = expert.astype(jnp.float32) * cap + jnp.sum(earlier * onehot, axis=0, keepdims=True)
    slot_rows = lax.broadcasted_iota(jnp.int32, (slots, count), 0).astype(jnp.float32)
    placing = (slot_rows == target).astype(jnp.float32).astype(jnp.bfloat16)
    tok_send[...] = jnp.dot(
        placing, tok_ref[...], preferred_element_type=jnp.float32
    ).astype(jnp.bfloat16)
    pl.semaphore_wait(barrier, n)
    send_all(0, tok_send, rows)

    gate = to_column(gate_ref[...])
    scaled = (gate * grad_ref[...].astype(jnp.float32)).astype(jnp.bfloat16)
    grad_send[...] = jnp.dot(
        placing, scaled, preferred_element_type=jnp.float32
    ).astype(jnp.bfloat16)
    send_all(1, grad_send, grads)
    slot_cols = lax.broadcasted_iota(jnp.int32, (count, slots), 1).astype(jnp.float32)
    placing_t[...] = (slot_cols == to_column(target)).astype(jnp.float32).astype(jnp.bfloat16)

    share(0, tok_send, rows)
    up_copy.wait()

    @pl.loop(0, units // CHUNK)
    def _(c):
        cols = pl.ds(pl.multiple_of(c * CHUNK, CHUNK), CHUNK)
        pre = jnp.dot(rows[...], up[:, cols], preferred_element_type=jnp.float32)
        square = pre * pre
        bend = jnp.tanh(SCALE * pre * (1.0 + CUBIC * square))
        half = 0.5 + 0.5 * bend
        hidden[:, cols] = (pre * half).astype(jnp.bfloat16)
        slope[:, cols] = half + (0.5 * SCALE) * pre * (1.0 - bend * bend) * (
            1.0 + (3.0 * CUBIC) * square
        )

    down_copy.wait()

    def merge(kind, product):
        @pl.loop(0, width // CHUNK)
        def _(c):
            cols = pl.ds(pl.multiple_of(c * CHUNK, CHUNK), CHUNK)
            merge_send[kind, :, cols] = product(slots, cols).astype(jnp.bfloat16)

        swap = remote(
            merge_send.at[kind],
            merge_recv.at[kind],
            merge_ssem.at[kind],
            merge_rsem.at[kind],
            partner,
        )
        swap.start()

        @pl.loop(0, width // CHUNK)
        def _(c):
            cols = pl.ds(pl.multiple_of(c * CHUNK, CHUNK), CHUNK)
            mine[:, cols] = product(0, cols)

        swap.wait_recv()
        ret_send[kind] = (mine[...] + merge_recv[kind].astype(jnp.float32)).astype(jnp.bfloat16)
        send_all(2 + kind, ret_send.at[kind], ret_recv.at[kind])

    def out_product(start, cols):
        return jnp.dot(
            hidden[start : start + slots, :], down[:, cols], preferred_element_type=jnp.float32
        )

    merge(0, out_product)

    share(1, grad_send, grads)
    across = (((1,), (1,)), ((), ()))

    @pl.loop(0, units // CHUNK)
    def _(c):
        cols = pl.ds(pl.multiple_of(c * CHUNK, CHUNK), CHUNK)
        dhid = lax.dot_general(
            grads[...], down[cols, :], across, preferred_element_type=jnp.float32
        )
        dpre[:, cols] = (dhid * slope[:, cols]).astype(jnp.bfloat16)

    def in_product(start, cols):
        return lax.dot_general(
            dpre[start : start + slots, :],
            up[cols, :],
            across,
            preferred_element_type=jnp.float32,
        )

    merge(1, in_product)

    rows_t[...] = rows[...].T

    @pl.loop(0, units // CHUNK)
    def _(c):
        cols = pl.ds(pl.multiple_of(c * CHUNK, CHUNK), CHUNK)
        ugrad_ref[0, :, cols] = jnp.dot(
            rows_t[...], dpre[:, cols], preferred_element_type=jnp.float32
        ).astype(jnp.bfloat16)
        dgrad_ref[0, cols, :] = lax.dot_general(
            hidden[:, cols],
            grads[...],
            (((0,), (0,)), ((), ())),
            preferred_element_type=jnp.float32,
        ).astype(jnp.bfloat16)

    def collect(kind):
        @pl.loop(1, n)
        def _(k):
            wait_block(2 + kind, ret_send.at[kind], ret_recv.at[kind], lax.rem(me + k, n))

        return jnp.dot(placing_t[...], ret_recv[kind], preferred_element_type=jnp.float32)

    returned = collect(0)
    out_ref[...] = (to_column(gate_ref[...]) * returned).astype(jnp.bfloat16)
    dots = jnp.sum(grad_ref[...].astype(jnp.float32) * returned, axis=1, keepdims=True)
    pgrad_ref[...] = jnp.sum(jnp.where(eye, dots, 0.0), axis=0, keepdims=True)
    tgrad_ref[...] = collect(1).astype(jnp.bfloat16)

    @pl.loop(1, n)
    def _(k):
        peer = lax.rem(me + k, n)
        exchange(0, tok_send, rows, peer, me).wait_send()
        exchange(1, grad_send, grads, peer, me).wait_send()
        exchange(2, ret_send.at[0], ret_recv.at[0], peer, me).wait_send()
        exchange(3, ret_send.at[1], ret_recv.at[1], peer, me).wait_send()

    @pl.loop(0, n)
    def _(k):
        forward(0, rows, k).wait_send()
        forward(1, grads, k).wait_send()

    for kind in range(2):
        remote(
            merge_send.at[kind],
            merge_recv.at[kind],
            merge_ssem.at[kind],
            merge_rsem.at[kind],
            partner,
        ).wait_send()


def local_fused(tokens, routing, gate_prob, up_weight, down_weight, out_grad):
    n = lax.axis_size("ep")
    count, width = tokens.shape
    units = up_weight.shape[2]
    cap = 2 * count // n
    slots = n * cap
    low, wide = jnp.bfloat16, jnp.float32
    vmem = pl.BlockSpec(memory_space=pltpu.VMEM)
    anywhere = pl.BlockSpec(memory_space=pl.ANY)
    dma = pltpu.SemaphoreType.DMA
    output, token_grad, prob_grad, up_grad, down_grad = pl.pallas_call(
        functools.partial(kernel, n, cap),
        out_shape=(
            jax.ShapeDtypeStruct((count, width), low),
            jax.ShapeDtypeStruct((count, width), low),
            jax.ShapeDtypeStruct((1, count), wide),
            jax.ShapeDtypeStruct(up_weight.shape, low),
            jax.ShapeDtypeStruct(down_weight.shape, low),
        ),
        in_specs=[vmem, vmem, vmem, anywhere, anywhere, vmem],
        out_specs=(vmem,) * 5,
        scratch_shapes=[
            pltpu.VMEM((width, units), low),
            pltpu.VMEM((units, width), low),
            pltpu.VMEM((slots, width), low),
            pltpu.VMEM((slots, width), low),
            pltpu.VMEM((2 * slots, width), low),
            pltpu.VMEM((2 * slots, width), low),
            pltpu.VMEM((width, 2 * slots), low),
            pltpu.VMEM((2 * slots, units), low),
            pltpu.VMEM((2 * slots, units), wide),
            pltpu.VMEM((2 * slots, units), low),
            pltpu.VMEM((slots, width), wide),
            pltpu.VMEM((2, slots, width), low),
            pltpu.VMEM((2, slots, width), low),
            pltpu.VMEM((2, slots, width), low),
            pltpu.VMEM((2, slots, width), low),
            pltpu.VMEM((count, slots), low),
            dma((2,)),
            dma((4, n)),
            dma((4, n)),
            dma((2, n)),
            dma((2, n)),
            dma((2,)),
            dma((2,)),
        ],
        compiler_params=pltpu.CompilerParams(
            collective_id=0, has_side_effects=True, vmem_limit_bytes=44 << 20
        ),
        cost_estimate=pl.CostEstimate(
            flops=12 * 2 * slots * width * units,
            bytes_accessed=8 * width * units,
            transcendentals=2 * slots * units,
        ),
    )(
        tokens,
        routing.reshape(1, count),
        gate_prob.reshape(1, count),
        up_weight,
        down_weight,
        out_grad,
    )
    return (output, token_grad, prob_grad.reshape(count), up_grad, down_grad)


def local(tokens, routing, gate_prob, up_weight, down_weight, out_grad):
    n = lax.axis_size("ep")
    count, width = tokens.shape
    fits = (
        up_weight.shape[0] == 1
        and lax.axis_size("dp") == 2
        and (2 * count // n) % TILE == 0
        and (2 * count) % n == 0
        and up_weight.shape[2] % CHUNK == 0
        and width % CHUNK == 0
    )
    run = local_fused if fits else local_plain
    return run(tokens, routing, gate_prob, up_weight, down_weight, out_grad)


def solution(mesh):
    placed = (
        P(("ep", "dp"), None),
        P(("ep", "dp"), None),
        P(("ep", "dp")),
        P("ep", None, "dp"),
        P("ep", "dp", None),
        P(("ep", "dp"), None),
    )
    return jax.shard_map(
        local,
        mesh=mesh,
        in_specs=placed,
        out_specs=(
            P(("ep", "dp"), None),
            P(("ep", "dp"), None),
            P(("ep", "dp")),
            P("ep", None, "dp"),
            P("ep", "dp", None),
        ),
        check_vma=False,
    )
```

```python
import functools

import jax
import jax.numpy as jnp
from jax import lax
from jax.experimental import pallas as pl
from jax.experimental.pallas import tpu as pltpu
from jax.sharding import PartitionSpec as P


def local_plain(tokens, routing, gate_prob, up_weight, down_weight, out_grad):
    token_count = tokens.shape[0]
    local_experts = up_weight.shape[0]
    peer_count = lax.axis_size("ep")
    experts = local_experts * peer_count
    capacity = max(2, 2 * token_count // experts)
    slot_count = experts * capacity
    expert = routing[:, 0]
    onehot = (expert[:, None] == jnp.arange(experts, dtype=jnp.int32)[None, :]).astype(jnp.int32)
    ranking = jnp.sum((jnp.cumsum(onehot, axis=0) - onehot) * onehot, axis=1)
    target = expert * capacity + ranking
    placing = (jnp.arange(slot_count, dtype=jnp.int32)[:, None] == target[None, :]).astype(
        jnp.bfloat16
    )

    def dispatch(values):
        packed = jnp.dot(placing, values, preferred_element_type=jnp.float32).astype(jnp.bfloat16)
        return packed.reshape(experts, capacity, values.shape[1])

    def collect(returned):
        flat = returned.reshape(slot_count, returned.shape[2])
        return jnp.einsum("st,sd->td", placing, flat, preferred_element_type=jnp.float32)

    grad_wide = out_grad.astype(jnp.float32)
    scaled = (gate_prob[:, None] * grad_wide).astype(jnp.bfloat16)
    sent_rows = lax.all_to_all(dispatch(tokens), "ep", split_axis=0, concat_axis=1, tiled=True)
    expert_rows = lax.all_gather(sent_rows, "dp", axis=1, tiled=True)
    up_full, down_full = (up_weight, down_weight)
    preact = jnp.einsum("erd,edf->erf", expert_rows, up_full, preferred_element_type=jnp.float32)
    activated, back_fn = jax.vjp(jax.nn.gelu, preact)
    hidden = activated.astype(jnp.bfloat16)
    partial_out = jnp.einsum("erf,efd->erd", hidden, down_full, preferred_element_type=jnp.float32)
    merged = lax.psum_scatter(partial_out, "dp", scatter_dimension=1, tiled=True)
    expert_out = lax.all_to_all(
        merged.astype(jnp.bfloat16), "ep", split_axis=1, concat_axis=0, tiled=True
    )
    expert_tok = collect(expert_out)
    output = (gate_prob[:, None] * expert_tok).astype(jnp.bfloat16)
    prob_grad = jnp.sum(grad_wide * expert_tok, axis=1)
    sent_grads = lax.all_to_all(dispatch(scaled), "ep", split_axis=0, concat_axis=1, tiled=True)
    grad_rows = lax.all_gather(sent_grads, "dp", axis=1, tiled=True)
    hidden_grad = jnp.einsum(
        "erd,efd->erf", grad_rows, down_full, preferred_element_type=jnp.float32
    )
    preact_grad = back_fn(hidden_grad)[0].astype(jnp.bfloat16)
    partial_input = jnp.einsum(
        "erf,edf->erd", preact_grad, up_full, preferred_element_type=jnp.float32
    )
    up_sum = jnp.einsum(
        "erd,erf->edf", expert_rows, preact_grad, preferred_element_type=jnp.float32
    )
    down_sum = jnp.einsum("erf,erd->efd", hidden, grad_rows, preferred_element_type=jnp.float32)
    input_rows = lax.psum_scatter(partial_input, "dp", scatter_dimension=1, tiled=True)
    up_grad = up_sum.astype(jnp.bfloat16)
    down_grad = down_sum.astype(jnp.bfloat16)
    returned = lax.all_to_all(
        input_rows.astype(jnp.bfloat16), "ep", split_axis=1, concat_axis=0, tiled=True
    )
    token_grad = collect(returned).astype(jnp.bfloat16)
    return (output, token_grad, prob_grad, up_grad, down_grad)


MESH = pl.DeviceIdType.MESH
TILE = 16
CHUNK = 256
SCALE = 0.7978845608028654
CUBIC = 0.044715


def row_block(start, size):
    return pl.ds(pl.multiple_of(start, TILE), size)


def kernel(
    n,
    cap,
    tok_hbm,
    route_hbm,
    gate_hbm,
    up_hbm,
    down_hbm,
    grad_hbm,
    out_ref,
    tgrad_ref,
    pgrad_ref,
    ugrad_hbm,
    dgrad_hbm,
    ugrad_ref,
    dgrad_ref,
    tok_ref,
    route_ref,
    gate_ref,
    grad_ref,
    up,
    down,
    tok_send,
    grad_send,
    rows,
    grads,
    rows_t,
    hidden,
    slope,
    dpre,
    mine,
    merge_send,
    merge_recv,
    ret_send,
    ret_recv,
    placing_t,
    weight_sem,
    ep_send,
    ep_recv,
    dp_send,
    dp_recv,
    merge_ssem,
    merge_rsem,
):
    me, core = lax.axis_index("ep"), lax.axis_index("dp")
    partner = (me, 1 - core)
    slots = n * cap
    count, width = tok_ref.shape
    units = up.shape[1]

    staged = [
        pltpu.make_async_copy(far, near, weight_sem.at[2 + i])
        for i, (far, near) in enumerate(
            (
                (route_hbm, route_ref),
                (tok_hbm, tok_ref),
                (gate_hbm, gate_ref),
                (grad_hbm, grad_ref),
            )
        )
    ]
    for copy in staged:
        copy.start()
    barrier = pltpu.get_barrier_semaphore()

    @pl.loop(1, n)
    def _(k):
        pl.semaphore_signal(
            barrier, inc=1, device_id=(lax.rem(me + k, n), core), device_id_type=MESH
        )

    pl.semaphore_signal(barrier, inc=1, device_id=partner, device_id_type=MESH)
    up_copy = pltpu.make_async_copy(up_hbm.at[0], up, weight_sem.at[0])
    down_copy = pltpu.make_async_copy(down_hbm.at[0], down, weight_sem.at[1])
    up_copy.start()
    down_copy.start()

    def remote(src, dst, ssem, rsem, device):
        return pltpu.make_async_remote_copy(
            src_ref=src,
            dst_ref=dst,
            send_sem=ssem,
            recv_sem=rsem,
            device_id=device,
            device_id_type=MESH,
        )

    def exchange(kind, src, dst, peer, slot):
        return remote(
            src.at[row_block(peer * cap, cap)],
            dst.at[row_block(slot * cap, cap)],
            ep_send.at[kind, peer],
            ep_recv.at[kind, slot],
            (peer, core),
        )

    def send_all(kind, src, dst):
        @pl.loop(1, n)
        def _(k):
            exchange(kind, src, dst, lax.rem(me + k, n), me).start()

        dst[row_block(me * cap, cap), :] = src[row_block(me * cap, cap), :]

    def wait_block(kind, src, dst, source):
        exchange(kind, src, dst, source, source).wait_recv()

    def forward(kind, buf, source):
        return remote(
            buf.at[row_block(source * cap, cap)],
            buf.at[row_block(slots + source * cap, cap)],
            dp_send.at[kind, source],
            dp_recv.at[kind, source],
            partner,
        )

    def share(kind, src, dst):
        forward(kind, dst, me).start()

        @pl.loop(1, n)
        def _(k):
            source = lax.rem(me + k, n)
            wait_block(kind, src, dst, source)
            forward(kind, dst, source).start()

    def shared(kind, dst):
        @pl.loop(0, n)
        def _(k):
            forward(kind, dst, k).wait_recv()

    eye = lax.broadcasted_iota(jnp.int32, (count, count), 0) == lax.broadcasted_iota(
        jnp.int32, (count, count), 1
    )

    def to_column(row):
        return jnp.sum(jnp.where(eye, row, 0.0), axis=1, keepdims=True)

    staged[0].wait()
    expert = route_ref[...]
    onehot = (lax.broadcasted_iota(jnp.int32, (n, count), 0) == expert).astype(jnp.float32)
    before = (
        lax.broadcasted_iota(jnp.int32, (count, count), 0)
        < lax.broadcasted_iota(jnp.int32, (count, count), 1)
    ).astype(jnp.float32)
    earlier = jnp.dot(
        onehot.astype(jnp.bfloat16),
        before.astype(jnp.bfloat16),
        preferred_element_type=jnp.float32,
    )
    target = expert.astype(jnp.float32) * cap + jnp.sum(earlier * onehot, axis=0, keepdims=True)
    slot_rows = lax.broadcasted_iota(jnp.int32, (slots, count), 0).astype(jnp.float32)
    placing = (slot_rows == target).astype(jnp.float32).astype(jnp.bfloat16)
    staged[1].wait()
    tok_send[...] = jnp.dot(
        placing, tok_ref[...], preferred_element_type=jnp.float32
    ).astype(jnp.bfloat16)
    pl.semaphore_wait(barrier, n)
    send_all(0, tok_send, rows)

    staged[2].wait()
    staged[3].wait()
    gate = to_column(gate_ref[...])
    scaled = (gate * grad_ref[...].astype(jnp.float32)).astype(jnp.bfloat16)
    grad_send[...] = jnp.dot(
        placing, scaled, preferred_element_type=jnp.float32
    ).astype(jnp.bfloat16)
    send_all(1, grad_send, grads)
    slot_cols = lax.broadcasted_iota(jnp.int32, (count, slots), 1).astype(jnp.float32)
    placing_t[...] = (slot_cols == to_column(target)).astype(jnp.float32).astype(jnp.bfloat16)

    share(0, tok_send, rows)
    shared(0, rows)
    up_copy.wait()

    @pl.loop(0, units // CHUNK)
    def _(c):
        cols = pl.ds(pl.multiple_of(c * CHUNK, CHUNK), CHUNK)
        pre = jnp.dot(rows[...], up[:, cols], preferred_element_type=jnp.float32)
        square = pre * pre
        bend = jnp.tanh(SCALE * pre * (1.0 + CUBIC * square))
        half = 0.5 + 0.5 * bend
        hidden[:, cols] = (pre * half).astype(jnp.bfloat16)
        slope[:, cols] = half + (0.5 * SCALE) * pre * (1.0 - bend * bend) * (
            1.0 + (3.0 * CUBIC) * square
        )

    down_copy.wait()

    def merge(kind, product, meanwhile):
        @pl.loop(0, width // CHUNK)
        def _(c):
            cols = pl.ds(pl.multiple_of(c * CHUNK, CHUNK), CHUNK)
            merge_send[kind, :, cols] = product(slots, cols).astype(jnp.bfloat16)

        swap = remote(
            merge_send.at[kind],
            merge_recv.at[kind],
            merge_ssem.at[kind],
            merge_rsem.at[kind],
            partner,
        )
        swap.start()

        @pl.loop(0, width // CHUNK)
        def _(c):
            cols = pl.ds(pl.multiple_of(c * CHUNK, CHUNK), CHUNK)
            mine[:, cols] = product(0, cols)

        meanwhile()
        swap.wait_recv()
        ret_send[kind] = (mine[...] + merge_recv[kind].astype(jnp.float32)).astype(jnp.bfloat16)
        send_all(2 + kind, ret_send.at[kind], ret_recv.at[kind])

    def out_product(start, cols):
        return jnp.dot(
            hidden[start : start + slots, :], down[:, cols], preferred_element_type=jnp.float32
        )

    merge(0, out_product, lambda: share(1, grad_send, grads))

    shared(1, grads)
    across = (((1,), (1,)), ((), ()))

    @pl.loop(0, units // CHUNK)
    def _(c):
        cols = pl.ds(pl.multiple_of(c * CHUNK, CHUNK), CHUNK)
        dhid = lax.dot_general(
            grads[...], down[cols, :], across, preferred_element_type=jnp.float32
        )
        dpre[:, cols] = (dhid * slope[:, cols]).astype(jnp.bfloat16)

    def in_product(start, cols):
        return lax.dot_general(
            dpre[start : start + slots, :],
            up[cols, :],
            across,
            preferred_element_type=jnp.float32,
        )

    merge(1, in_product, lambda: None)

    rows_t[...] = rows[...].T

    @pl.loop(0, units // CHUNK)
    def _(c):
        cols = pl.ds(pl.multiple_of(c * CHUNK, CHUNK), CHUNK)
        ugrad_ref[:, cols] = jnp.dot(
            rows_t[...], dpre[:, cols], preferred_element_type=jnp.float32
        ).astype(jnp.bfloat16)
        dgrad_ref[cols, :] = lax.dot_general(
            hidden[:, cols],
            grads[...],
            (((0,), (0,)), ((), ())),
            preferred_element_type=jnp.float32,
        ).astype(jnp.bfloat16)

    writes = (
        pltpu.make_async_copy(ugrad_ref, ugrad_hbm.at[0], weight_sem.at[6]),
        pltpu.make_async_copy(dgrad_ref, dgrad_hbm.at[0], weight_sem.at[7]),
    )
    for write in writes:
        write.start()

    def collect(kind):
        @pl.loop(1, n)
        def _(k):
            wait_block(2 + kind, ret_send.at[kind], ret_recv.at[kind], lax.rem(me + k, n))

        return jnp.dot(placing_t[...], ret_recv[kind], preferred_element_type=jnp.float32)

    returned = collect(0)
    out_ref[...] = (to_column(gate_ref[...]) * returned).astype(jnp.bfloat16)
    dots = jnp.sum(grad_ref[...].astype(jnp.float32) * returned, axis=1, keepdims=True)
    pgrad_ref[...] = jnp.sum(jnp.where(eye, dots, 0.0), axis=0, keepdims=True)
    tgrad_ref[...] = collect(1).astype(jnp.bfloat16)

    @pl.loop(1, n)
    def _(k):
        peer = lax.rem(me + k, n)
        exchange(0, tok_send, rows, peer, me).wait_send()
        exchange(1, grad_send, grads, peer, me).wait_send()
        exchange(2, ret_send.at[0], ret_recv.at[0], peer, me).wait_send()
        exchange(3, ret_send.at[1], ret_recv.at[1], peer, me).wait_send()

    @pl.loop(0, n)
    def _(k):
        forward(0, rows, k).wait_send()
        forward(1, grads, k).wait_send()

    for write in writes:
        write.wait()
    for kind in range(2):
        remote(
            merge_send.at[kind],
            merge_recv.at[kind],
            merge_ssem.at[kind],
            merge_rsem.at[kind],
            partner,
        ).wait_send()


def local_fused(tokens, routing, gate_prob, up_weight, down_weight, out_grad):
    n = lax.axis_size("ep")
    count, width = tokens.shape
    units = up_weight.shape[2]
    cap = 2 * count // n
    slots = n * cap
    low, wide = jnp.bfloat16, jnp.float32
    vmem = pl.BlockSpec(memory_space=pltpu.VMEM)
    far = pl.BlockSpec(memory_space=pltpu.HBM)
    dma = pltpu.SemaphoreType.DMA
    output, token_grad, prob_grad, up_grad, down_grad = pl.pallas_call(
        functools.partial(kernel, n, cap),
        out_shape=(
            jax.ShapeDtypeStruct((count, width), low),
            jax.ShapeDtypeStruct((count, width), low),
            jax.ShapeDtypeStruct((1, count), wide),
            jax.ShapeDtypeStruct(up_weight.shape, low),
            jax.ShapeDtypeStruct(down_weight.shape, low),
        ),
        in_specs=[far] * 6,
        out_specs=(vmem, vmem, vmem, far, far),
        scratch_shapes=[
            pltpu.VMEM((width, units), low),
            pltpu.VMEM((units, width), low),
            pltpu.VMEM((count, width), low),
            pltpu.VMEM((1, count), jnp.int32),
            pltpu.VMEM((1, count), wide),
            pltpu.VMEM((count, width), low),
            pltpu.VMEM((width, units), low),
            pltpu.VMEM((units, width), low),
            pltpu.VMEM((slots, width), low),
            pltpu.VMEM((slots, width), low),
            pltpu.VMEM((2 * slots, width), low),
            pltpu.VMEM((2 * slots, width), low),
            pltpu.VMEM((width, 2 * slots), low),
            pltpu.VMEM((2 * slots, units), low),
            pltpu.VMEM((2 * slots, units), wide),
            pltpu.VMEM((2 * slots, units), low),
            pltpu.VMEM((slots, width), wide),
            pltpu.VMEM((2, slots, width), low),
            pltpu.VMEM((2, slots, width), low),
            pltpu.VMEM((2, slots, width), low),
            pltpu.VMEM((2, slots, width), low),
            pltpu.VMEM((count, slots), low),
            dma((8,)),
            dma((4, n)),
            dma((4, n)),
            dma((2, n)),
            dma((2, n)),
            dma((2,)),
            dma((2,)),
        ],
        compiler_params=pltpu.CompilerParams(
            collective_id=0, has_side_effects=True, vmem_limit_bytes=58 << 20
        ),
        cost_estimate=pl.CostEstimate(
            flops=12 * 2 * slots * width * units,
            bytes_accessed=8 * width * units,
            transcendentals=2 * slots * units,
        ),
    )(
        tokens,
        routing.reshape(1, count),
        gate_prob.reshape(1, count),
        up_weight,
        down_weight,
        out_grad,
    )
    return (output, token_grad, prob_grad.reshape(count), up_grad, down_grad)


def local(tokens, routing, gate_prob, up_weight, down_weight, out_grad):
    n = lax.axis_size("ep")
    count, width = tokens.shape
    fits = (
        up_weight.shape[0] == 1
        and lax.axis_size("dp") == 2
        and (2 * count // n) % TILE == 0
        and (2 * count) % n == 0
        and up_weight.shape[2] % CHUNK == 0
        and width % CHUNK == 0
    )
    run = local_fused if fits else local_plain
    return run(tokens, routing, gate_prob, up_weight, down_weight, out_grad)


def solution(mesh):
    placed = (
        P(("ep", "dp"), None),
        P(("ep", "dp"), None),
        P(("ep", "dp")),
        P("ep", None, "dp"),
        P("ep", "dp", None),
        P(("ep", "dp"), None),
    )
    return jax.shard_map(
        local,
        mesh=mesh,
        in_specs=placed,
        out_specs=(
            P(("ep", "dp"), None),
            P(("ep", "dp"), None),
            P(("ep", "dp")),
            P("ep", None, "dp"),
            P("ep", "dp", None),
        ),
        check_vma=False,
    )
```

```python
import functools

import jax
import jax.numpy as jnp
from jax import lax
from jax.experimental import pallas as pl
from jax.experimental.pallas import tpu as pltpu
from jax.sharding import PartitionSpec as P


def local_plain(tokens, routing, gate_prob, up_weight, down_weight, out_grad):
    token_count = tokens.shape[0]
    local_experts = up_weight.shape[0]
    peer_count = lax.axis_size("ep")
    experts = local_experts * peer_count
    capacity = max(2, 2 * token_count // experts)
    slot_count = experts * capacity
    expert = routing[:, 0]
    onehot = (expert[:, None] == jnp.arange(experts, dtype=jnp.int32)[None, :]).astype(jnp.int32)
    ranking = jnp.sum((jnp.cumsum(onehot, axis=0) - onehot) * onehot, axis=1)
    target = expert * capacity + ranking
    placing = (jnp.arange(slot_count, dtype=jnp.int32)[:, None] == target[None, :]).astype(
        jnp.bfloat16
    )

    def dispatch(values):
        packed = jnp.dot(placing, values, preferred_element_type=jnp.float32).astype(jnp.bfloat16)
        return packed.reshape(experts, capacity, values.shape[1])

    def collect(returned):
        flat = returned.reshape(slot_count, returned.shape[2])
        return jnp.einsum("st,sd->td", placing, flat, preferred_element_type=jnp.float32)

    grad_wide = out_grad.astype(jnp.float32)
    scaled = (gate_prob[:, None] * grad_wide).astype(jnp.bfloat16)
    sent_rows = lax.all_to_all(dispatch(tokens), "ep", split_axis=0, concat_axis=1, tiled=True)
    expert_rows = lax.all_gather(sent_rows, "dp", axis=1, tiled=True)
    up_full, down_full = (up_weight, down_weight)
    preact = jnp.einsum("erd,edf->erf", expert_rows, up_full, preferred_element_type=jnp.float32)
    activated, back_fn = jax.vjp(jax.nn.gelu, preact)
    hidden = activated.astype(jnp.bfloat16)
    partial_out = jnp.einsum("erf,efd->erd", hidden, down_full, preferred_element_type=jnp.float32)
    merged = lax.psum_scatter(partial_out, "dp", scatter_dimension=1, tiled=True)
    expert_out = lax.all_to_all(
        merged.astype(jnp.bfloat16), "ep", split_axis=1, concat_axis=0, tiled=True
    )
    expert_tok = collect(expert_out)
    output = (gate_prob[:, None] * expert_tok).astype(jnp.bfloat16)
    prob_grad = jnp.sum(grad_wide * expert_tok, axis=1)
    sent_grads = lax.all_to_all(dispatch(scaled), "ep", split_axis=0, concat_axis=1, tiled=True)
    grad_rows = lax.all_gather(sent_grads, "dp", axis=1, tiled=True)
    hidden_grad = jnp.einsum(
        "erd,efd->erf", grad_rows, down_full, preferred_element_type=jnp.float32
    )
    preact_grad = back_fn(hidden_grad)[0].astype(jnp.bfloat16)
    partial_input = jnp.einsum(
        "erf,edf->erd", preact_grad, up_full, preferred_element_type=jnp.float32
    )
    up_sum = jnp.einsum(
        "erd,erf->edf", expert_rows, preact_grad, preferred_element_type=jnp.float32
    )
    down_sum = jnp.einsum("erf,erd->efd", hidden, grad_rows, preferred_element_type=jnp.float32)
    input_rows = lax.psum_scatter(partial_input, "dp", scatter_dimension=1, tiled=True)
    up_grad = up_sum.astype(jnp.bfloat16)
    down_grad = down_sum.astype(jnp.bfloat16)
    returned = lax.all_to_all(
        input_rows.astype(jnp.bfloat16), "ep", split_axis=1, concat_axis=0, tiled=True
    )
    token_grad = collect(returned).astype(jnp.bfloat16)
    return (output, token_grad, prob_grad, up_grad, down_grad)


MESH = pl.DeviceIdType.MESH
TILE = 16
CHUNK = 256
SCALE = 0.7978845608028654
CUBIC = 0.044715


def row_block(start, size):
    return pl.ds(pl.multiple_of(start, TILE), size)


def kernel(
    n,
    cap,
    tok_hbm,
    route_hbm,
    gate_hbm,
    up_hbm,
    down_hbm,
    grad_hbm,
    out_ref,
    tgrad_ref,
    pgrad_ref,
    ugrad_ref,
    dgrad_ref,
    tok_ref,
    route_ref,
    gate_ref,
    grad_ref,
    up,
    down,
    tok_send,
    grad_send,
    rows,
    grads,
    rows_t,
    hidden,
    slope,
    dpre,
    mine,
    merge_send,
    merge_recv,
    ret_send,
    ret_recv,
    placing_t,
    weight_sem,
    ep_send,
    ep_recv,
    dp_send,
    dp_recv,
    merge_ssem,
    merge_rsem,
):
    me, core = lax.axis_index("ep"), lax.axis_index("dp")
    partner = (me, 1 - core)
    slots = n * cap
    count, width = tok_ref.shape
    units = up.shape[1]

    staged = [
        pltpu.make_async_copy(far, near, weight_sem.at[2 + i])
        for i, (far, near) in enumerate(
            (
                (route_hbm, route_ref),
                (tok_hbm, tok_ref),
                (gate_hbm, gate_ref),
                (grad_hbm, grad_ref),
            )
        )
    ]
    for copy in staged:
        copy.start()
    barrier = pltpu.get_barrier_semaphore()

    @pl.loop(1, n)
    def _(k):
        pl.semaphore_signal(
            barrier, inc=1, device_id=(lax.rem(me + k, n), core), device_id_type=MESH
        )

    pl.semaphore_signal(barrier, inc=1, device_id=partner, device_id_type=MESH)
    up_copy = pltpu.make_async_copy(up_hbm.at[0], up, weight_sem.at[0])
    down_copy = pltpu.make_async_copy(down_hbm.at[0], down, weight_sem.at[1])
    up_copy.start()
    down_copy.start()

    def remote(src, dst, ssem, rsem, device):
        return pltpu.make_async_remote_copy(
            src_ref=src,
            dst_ref=dst,
            send_sem=ssem,
            recv_sem=rsem,
            device_id=device,
            device_id_type=MESH,
        )

    def exchange(kind, src, dst, peer, slot):
        return remote(
            src.at[row_block(peer * cap, cap)],
            dst.at[row_block(slot * cap, cap)],
            ep_send.at[kind, peer],
            ep_recv.at[kind, slot],
            (peer, core),
        )

    def send_all(kind, src, dst):
        @pl.loop(1, n)
        def _(k):
            exchange(kind, src, dst, lax.rem(me + k, n), me).start()

        dst[row_block(me * cap, cap), :] = src[row_block(me * cap, cap), :]

    def wait_block(kind, src, dst, source):
        exchange(kind, src, dst, source, source).wait_recv()

    def forward(kind, buf, source):
        return remote(
            buf.at[row_block(source * cap, cap)],
            buf.at[row_block(slots + source * cap, cap)],
            dp_send.at[kind, source],
            dp_recv.at[kind, source],
            partner,
        )

    def share(kind, src, dst, then):
        forward(kind, dst, me).start()

        @pl.loop(1, n)
        def _(k):
            source = lax.rem(me + k, n)
            wait_block(kind, src, dst, source)
            forward(kind, dst, source).start()
            then(k)

    def shared(kind, dst):
        @pl.loop(0, n)
        def _(k):
            forward(kind, dst, k).wait_recv()

    eye = lax.broadcasted_iota(jnp.int32, (count, count), 0) == lax.broadcasted_iota(
        jnp.int32, (count, count), 1
    )

    def to_column(row):
        return jnp.sum(jnp.where(eye, row, 0.0), axis=1, keepdims=True)

    staged[0].wait()
    expert = route_ref[...]
    onehot = (lax.broadcasted_iota(jnp.int32, (n, count), 0) == expert).astype(jnp.float32)
    before = (
        lax.broadcasted_iota(jnp.int32, (count, count), 0)
        < lax.broadcasted_iota(jnp.int32, (count, count), 1)
    ).astype(jnp.float32)
    earlier = jnp.dot(
        onehot.astype(jnp.bfloat16),
        before.astype(jnp.bfloat16),
        preferred_element_type=jnp.float32,
    )
    target = expert.astype(jnp.float32) * cap + jnp.sum(earlier * onehot, axis=0, keepdims=True)
    slot_rows = lax.broadcasted_iota(jnp.int32, (slots, count), 0).astype(jnp.float32)
    placing = (slot_rows == target).astype(jnp.float32).astype(jnp.bfloat16)
    staged[1].wait()
    tok_send[...] = jnp.dot(
        placing, tok_ref[...], preferred_element_type=jnp.float32
    ).astype(jnp.bfloat16)
    pl.semaphore_wait(barrier, n)
    send_all(0, tok_send, rows)

    staged[2].wait()
    staged[3].wait()
    gate = to_column(gate_ref[...])
    scaled = (gate * grad_ref[...].astype(jnp.float32)).astype(jnp.bfloat16)
    grad_send[...] = jnp.dot(
        placing, scaled, preferred_element_type=jnp.float32
    ).astype(jnp.bfloat16)
    grads[row_block(me * cap, cap), :] = grad_send[row_block(me * cap, cap), :]
    slot_cols = lax.broadcasted_iota(jnp.int32, (count, slots), 1).astype(jnp.float32)
    placing_t[...] = (slot_cols == to_column(target)).astype(jnp.float32).astype(jnp.bfloat16)

    def send_grads(k):
        exchange(1, grad_send, grads, lax.rem(me + k, n), me).start()

    share(0, tok_send, rows, send_grads)
    shared(0, rows)
    up_copy.wait()

    @pl.loop(0, units // CHUNK)
    def _(c):
        cols = pl.ds(pl.multiple_of(c * CHUNK, CHUNK), CHUNK)
        pre = jnp.dot(rows[...], up[:, cols], preferred_element_type=jnp.float32)
        square = pre * pre
        bend = jnp.tanh(SCALE * pre * (1.0 + CUBIC * square))
        half = 0.5 + 0.5 * bend
        hidden[:, cols] = (pre * half).astype(jnp.bfloat16)
        slope[:, cols] = half + (0.5 * SCALE) * pre * (1.0 - bend * bend) * (
            1.0 + (3.0 * CUBIC) * square
        )

    down_copy.wait()

    def merge(kind, product, meanwhile):
        @pl.loop(0, width // CHUNK)
        def _(c):
            cols = pl.ds(pl.multiple_of(c * CHUNK, CHUNK), CHUNK)
            merge_send[kind, :, cols] = product(slots, cols).astype(jnp.bfloat16)

        swap = remote(
            merge_send.at[kind],
            merge_recv.at[kind],
            merge_ssem.at[kind],
            merge_rsem.at[kind],
            partner,
        )
        swap.start()

        @pl.loop(0, width // CHUNK)
        def _(c):
            cols = pl.ds(pl.multiple_of(c * CHUNK, CHUNK), CHUNK)
            mine[:, cols] = product(0, cols)

        meanwhile()
        swap.wait_recv()
        ret_send[kind] = (mine[...] + merge_recv[kind].astype(jnp.float32)).astype(jnp.bfloat16)
        send_all(2 + kind, ret_send.at[kind], ret_recv.at[kind])

    def out_product(start, cols):
        return jnp.dot(
            hidden[start : start + slots, :], down[:, cols], preferred_element_type=jnp.float32
        )

    merge(0, out_product, lambda: share(1, grad_send, grads, lambda k: None))

    shared(1, grads)
    across = (((1,), (1,)), ((), ()))

    @pl.loop(0, units // CHUNK)
    def _(c):
        cols = pl.ds(pl.multiple_of(c * CHUNK, CHUNK), CHUNK)
        dhid = lax.dot_general(
            grads[...], down[cols, :], across, preferred_element_type=jnp.float32
        )
        dpre[:, cols] = (dhid * slope[:, cols]).astype(jnp.bfloat16)

    def in_product(start, cols):
        return lax.dot_general(
            dpre[start : start + slots, :],
            up[cols, :],
            across,
            preferred_element_type=jnp.float32,
        )

    merge(1, in_product, lambda: None)

    rows_t[...] = rows[...].T

    @pl.loop(0, units // CHUNK)
    def _(c):
        cols = pl.ds(pl.multiple_of(c * CHUNK, CHUNK), CHUNK)
        ugrad_ref[0, :, cols] = jnp.dot(
            rows_t[...], dpre[:, cols], preferred_element_type=jnp.float32
        ).astype(jnp.bfloat16)
        dgrad_ref[0, cols, :] = lax.dot_general(
            hidden[:, cols],
            grads[...],
            (((0,), (0,)), ((), ())),
            preferred_element_type=jnp.float32,
        ).astype(jnp.bfloat16)

    def collect(kind):
        @pl.loop(1, n)
        def _(k):
            wait_block(2 + kind, ret_send.at[kind], ret_recv.at[kind], lax.rem(me + k, n))

        return jnp.dot(placing_t[...], ret_recv[kind], preferred_element_type=jnp.float32)

    returned = collect(0)
    out_ref[...] = (to_column(gate_ref[...]) * returned).astype(jnp.bfloat16)
    dots = jnp.sum(grad_ref[...].astype(jnp.float32) * returned, axis=1, keepdims=True)
    pgrad_ref[...] = jnp.sum(jnp.where(eye, dots, 0.0), axis=0, keepdims=True)
    tgrad_ref[...] = collect(1).astype(jnp.bfloat16)

    @pl.loop(1, n)
    def _(k):
        peer = lax.rem(me + k, n)
        exchange(0, tok_send, rows, peer, me).wait_send()
        exchange(1, grad_send, grads, peer, me).wait_send()
        exchange(2, ret_send.at[0], ret_recv.at[0], peer, me).wait_send()
        exchange(3, ret_send.at[1], ret_recv.at[1], peer, me).wait_send()

    @pl.loop(0, n)
    def _(k):
        forward(0, rows, k).wait_send()
        forward(1, grads, k).wait_send()

    for kind in range(2):
        remote(
            merge_send.at[kind],
            merge_recv.at[kind],
            merge_ssem.at[kind],
            merge_rsem.at[kind],
            partner,
        ).wait_send()


def local_fused(tokens, routing, gate_prob, up_weight, down_weight, out_grad):
    n = lax.axis_size("ep")
    count, width = tokens.shape
    units = up_weight.shape[2]
    cap = 2 * count // n
    slots = n * cap
    low, wide = jnp.bfloat16, jnp.float32
    vmem = pl.BlockSpec(memory_space=pltpu.VMEM)
    far = pl.BlockSpec(memory_space=pltpu.HBM)
    dma = pltpu.SemaphoreType.DMA
    output, token_grad, prob_grad, up_grad, down_grad = pl.pallas_call(
        functools.partial(kernel, n, cap),
        out_shape=(
            jax.ShapeDtypeStruct((count, width), low),
            jax.ShapeDtypeStruct((count, width), low),
            jax.ShapeDtypeStruct((1, count), wide),
            jax.ShapeDtypeStruct(up_weight.shape, low),
            jax.ShapeDtypeStruct(down_weight.shape, low),
        ),
        in_specs=[far] * 6,
        out_specs=(vmem,) * 5,
        scratch_shapes=[
            pltpu.VMEM((count, width), low),
            pltpu.VMEM((1, count), jnp.int32),
            pltpu.VMEM((1, count), wide),
            pltpu.VMEM((count, width), low),
            pltpu.VMEM((width, units), low),
            pltpu.VMEM((units, width), low),
            pltpu.VMEM((slots, width), low),
            pltpu.VMEM((slots, width), low),
            pltpu.VMEM((2 * slots, width), low),
            pltpu.VMEM((2 * slots, width), low),
            pltpu.VMEM((width, 2 * slots), low),
            pltpu.VMEM((2 * slots, units), low),
            pltpu.VMEM((2 * slots, units), wide),
            pltpu.VMEM((2 * slots, units), low),
            pltpu.VMEM((slots, width), wide),
            pltpu.VMEM((2, slots, width), low),
            pltpu.VMEM((2, slots, width), low),
            pltpu.VMEM((2, slots, width), low),
            pltpu.VMEM((2, slots, width), low),
            pltpu.VMEM((count, slots), low),
            dma((6,)),
            dma((4, n)),
            dma((4, n)),
            dma((2, n)),
            dma((2, n)),
            dma((2,)),
            dma((2,)),
        ],
        compiler_params=pltpu.CompilerParams(
            collective_id=0, has_side_effects=True, vmem_limit_bytes=48 << 20
        ),
        cost_estimate=pl.CostEstimate(
            flops=12 * 2 * slots * width * units,
            bytes_accessed=8 * width * units,
            transcendentals=2 * slots * units,
        ),
    )(
        tokens,
        routing.reshape(1, count),
        gate_prob.reshape(1, count),
        up_weight,
        down_weight,
        out_grad,
    )
    return (output, token_grad, prob_grad.reshape(count), up_grad, down_grad)


def local(tokens, routing, gate_prob, up_weight, down_weight, out_grad):
    n = lax.axis_size("ep")
    count, width = tokens.shape
    fits = (
        up_weight.shape[0] == 1
        and lax.axis_size("dp") == 2
        and (2 * count // n) % TILE == 0
        and (2 * count) % n == 0
        and up_weight.shape[2] % CHUNK == 0
        and width % CHUNK == 0
    )
    run = local_fused if fits else local_plain
    return run(tokens, routing, gate_prob, up_weight, down_weight, out_grad)


def solution(mesh):
    placed = (
        P(("ep", "dp"), None),
        P(("ep", "dp"), None),
        P(("ep", "dp")),
        P("ep", None, "dp"),
        P("ep", "dp", None),
        P(("ep", "dp"), None),
    )
    return jax.shard_map(
        local,
        mesh=mesh,
        in_specs=placed,
        out_specs=(
            P(("ep", "dp"), None),
            P(("ep", "dp"), None),
            P(("ep", "dp")),
            P("ep", None, "dp"),
            P("ep", "dp", None),
        ),
        check_vma=False,
    )
```

```python
import functools

import jax
import jax.numpy as jnp
from jax import lax
from jax.experimental import pallas as pl
from jax.experimental.pallas import tpu as pltpu
from jax.sharding import PartitionSpec as P


def local_plain(tokens, routing, gate_prob, up_weight, down_weight, out_grad):
    token_count = tokens.shape[0]
    local_experts = up_weight.shape[0]
    peer_count = lax.axis_size("ep")
    experts = local_experts * peer_count
    capacity = max(2, 2 * token_count // experts)
    slot_count = experts * capacity
    expert = routing[:, 0]
    onehot = (expert[:, None] == jnp.arange(experts, dtype=jnp.int32)[None, :]).astype(jnp.int32)
    ranking = jnp.sum((jnp.cumsum(onehot, axis=0) - onehot) * onehot, axis=1)
    target = expert * capacity + ranking
    placing = (jnp.arange(slot_count, dtype=jnp.int32)[:, None] == target[None, :]).astype(
        jnp.bfloat16
    )

    def dispatch(values):
        packed = jnp.dot(placing, values, preferred_element_type=jnp.float32).astype(jnp.bfloat16)
        return packed.reshape(experts, capacity, values.shape[1])

    def collect(returned):
        flat = returned.reshape(slot_count, returned.shape[2])
        return jnp.einsum("st,sd->td", placing, flat, preferred_element_type=jnp.float32)

    grad_wide = out_grad.astype(jnp.float32)
    scaled = (gate_prob[:, None] * grad_wide).astype(jnp.bfloat16)
    sent_rows = lax.all_to_all(dispatch(tokens), "ep", split_axis=0, concat_axis=1, tiled=True)
    expert_rows = lax.all_gather(sent_rows, "dp", axis=1, tiled=True)
    up_full, down_full = (up_weight, down_weight)
    preact = jnp.einsum("erd,edf->erf", expert_rows, up_full, preferred_element_type=jnp.float32)
    activated, back_fn = jax.vjp(jax.nn.gelu, preact)
    hidden = activated.astype(jnp.bfloat16)
    partial_out = jnp.einsum("erf,efd->erd", hidden, down_full, preferred_element_type=jnp.float32)
    merged = lax.psum_scatter(partial_out, "dp", scatter_dimension=1, tiled=True)
    expert_out = lax.all_to_all(
        merged.astype(jnp.bfloat16), "ep", split_axis=1, concat_axis=0, tiled=True
    )
    expert_tok = collect(expert_out)
    output = (gate_prob[:, None] * expert_tok).astype(jnp.bfloat16)
    prob_grad = jnp.sum(grad_wide * expert_tok, axis=1)
    sent_grads = lax.all_to_all(dispatch(scaled), "ep", split_axis=0, concat_axis=1, tiled=True)
    grad_rows = lax.all_gather(sent_grads, "dp", axis=1, tiled=True)
    hidden_grad = jnp.einsum(
        "erd,efd->erf", grad_rows, down_full, preferred_element_type=jnp.float32
    )
    preact_grad = back_fn(hidden_grad)[0].astype(jnp.bfloat16)
    partial_input = jnp.einsum(
        "erf,edf->erd", preact_grad, up_full, preferred_element_type=jnp.float32
    )
    up_sum = jnp.einsum(
        "erd,erf->edf", expert_rows, preact_grad, preferred_element_type=jnp.float32
    )
    down_sum = jnp.einsum("erf,erd->efd", hidden, grad_rows, preferred_element_type=jnp.float32)
    input_rows = lax.psum_scatter(partial_input, "dp", scatter_dimension=1, tiled=True)
    up_grad = up_sum.astype(jnp.bfloat16)
    down_grad = down_sum.astype(jnp.bfloat16)
    returned = lax.all_to_all(
        input_rows.astype(jnp.bfloat16), "ep", split_axis=1, concat_axis=0, tiled=True
    )
    token_grad = collect(returned).astype(jnp.bfloat16)
    return (output, token_grad, prob_grad, up_grad, down_grad)


MESH = pl.DeviceIdType.MESH
TILE = 16
CHUNK = 256
SCALE = 0.7978845608028654
CUBIC = 0.044715


def row_block(start, size):
    return pl.ds(pl.multiple_of(start, TILE), size)


def kernel(
    n,
    cap,
    tok_hbm,
    route_hbm,
    gate_hbm,
    up_hbm,
    down_hbm,
    grad_hbm,
    out_ref,
    tgrad_ref,
    pgrad_ref,
    ugrad_ref,
    dgrad_ref,
    tok_ref,
    route_ref,
    gate_ref,
    grad_ref,
    up,
    down,
    tok_send,
    grad_send,
    rows,
    grads,
    rows_t,
    hidden,
    slope,
    dpre,
    mine,
    merge_send,
    merge_recv,
    ret_send,
    ret_recv,
    placing_t,
    weight_sem,
    ep_send,
    ep_recv,
    dp_send,
    dp_recv,
    merge_ssem,
    merge_rsem,
):
    me, core = lax.axis_index("ep"), lax.axis_index("dp")
    partner = (me, 1 - core)
    slots = n * cap
    count, width = tok_ref.shape
    units = up.shape[1]

    staged = [
        pltpu.make_async_copy(far, near, weight_sem.at[2 + i])
        for i, (far, near) in enumerate(
            (
                (route_hbm, route_ref),
                (tok_hbm, tok_ref),
                (gate_hbm, gate_ref),
                (grad_hbm, grad_ref),
            )
        )
    ]
    for copy in staged:
        copy.start()
    barrier = pltpu.get_barrier_semaphore()

    @pl.loop(1, n)
    def _(k):
        pl.semaphore_signal(
            barrier, inc=1, device_id=(lax.rem(me + k, n), core), device_id_type=MESH
        )

    pl.semaphore_signal(barrier, inc=1, device_id=partner, device_id_type=MESH)
    up_copy = pltpu.make_async_copy(up_hbm.at[0], up, weight_sem.at[0])
    down_copy = pltpu.make_async_copy(down_hbm.at[0], down, weight_sem.at[1])
    up_copy.start()
    down_copy.start()

    def remote(src, dst, ssem, rsem, device):
        return pltpu.make_async_remote_copy(
            src_ref=src,
            dst_ref=dst,
            send_sem=ssem,
            recv_sem=rsem,
            device_id=device,
            device_id_type=MESH,
        )

    def exchange(kind, src, dst, peer, slot):
        return remote(
            src.at[row_block(peer * cap, cap)],
            dst.at[row_block(slot * cap, cap)],
            ep_send.at[kind, peer],
            ep_recv.at[kind, slot],
            (peer, core),
        )

    def far_first(k):
        return 1 + lax.rem(k + n // 2 - 2, n - 1)

    def send_all(kind, src, dst):
        @pl.loop(1, n)
        def _(k):
            exchange(kind, src, dst, lax.rem(me + far_first(k), n), me).start()

        dst[row_block(me * cap, cap), :] = src[row_block(me * cap, cap), :]

    def wait_block(kind, src, dst, source):
        exchange(kind, src, dst, source, source).wait_recv()

    def forward(kind, buf, source):
        return remote(
            buf.at[row_block(source * cap, cap)],
            buf.at[row_block(slots + source * cap, cap)],
            dp_send.at[kind, source],
            dp_recv.at[kind, source],
            partner,
        )

    def share(kind, src, dst, then):
        forward(kind, dst, me).start()

        @pl.loop(1, n)
        def _(k):
            source = lax.rem(me + n - far_first(k), n)
            wait_block(kind, src, dst, source)
            forward(kind, dst, source).start()
            then(k)

    def shared(kind, dst):
        @pl.loop(0, n)
        def _(k):
            forward(kind, dst, k).wait_recv()

    eye = lax.broadcasted_iota(jnp.int32, (count, count), 0) == lax.broadcasted_iota(
        jnp.int32, (count, count), 1
    )

    def to_column(row):
        return jnp.sum(jnp.where(eye, row, 0.0), axis=1, keepdims=True)

    staged[0].wait()
    expert = route_ref[...]
    onehot = (lax.broadcasted_iota(jnp.int32, (n, count), 0) == expert).astype(jnp.float32)
    before = (
        lax.broadcasted_iota(jnp.int32, (count, count), 0)
        < lax.broadcasted_iota(jnp.int32, (count, count), 1)
    ).astype(jnp.float32)
    earlier = jnp.dot(
        onehot.astype(jnp.bfloat16),
        before.astype(jnp.bfloat16),
        preferred_element_type=jnp.float32,
    )
    target = expert.astype(jnp.float32) * cap + jnp.sum(earlier * onehot, axis=0, keepdims=True)
    slot_rows = lax.broadcasted_iota(jnp.int32, (slots, count), 0).astype(jnp.float32)
    placing = (slot_rows == target).astype(jnp.float32).astype(jnp.bfloat16)
    staged[1].wait()
    tok_send[...] = jnp.dot(
        placing, tok_ref[...], preferred_element_type=jnp.float32
    ).astype(jnp.bfloat16)
    pl.semaphore_wait(barrier, n)
    send_all(0, tok_send, rows)

    staged[2].wait()
    staged[3].wait()
    gate = to_column(gate_ref[...])
    scaled = (gate * grad_ref[...].astype(jnp.float32)).astype(jnp.bfloat16)
    grad_send[...] = jnp.dot(
        placing, scaled, preferred_element_type=jnp.float32
    ).astype(jnp.bfloat16)
    grads[row_block(me * cap, cap), :] = grad_send[row_block(me * cap, cap), :]
    slot_cols = lax.broadcasted_iota(jnp.int32, (count, slots), 1).astype(jnp.float32)
    placing_t[...] = (slot_cols == to_column(target)).astype(jnp.float32).astype(jnp.bfloat16)

    def send_grads(k):
        exchange(1, grad_send, grads, lax.rem(me + far_first(k), n), me).start()

    share(0, tok_send, rows, send_grads)
    shared(0, rows)
    up_copy.wait()

    @pl.loop(0, units // CHUNK)
    def _(c):
        cols = pl.ds(pl.multiple_of(c * CHUNK, CHUNK), CHUNK)
        pre = jnp.dot(rows[...], up[:, cols], preferred_element_type=jnp.float32)
        square = pre * pre
        bend = jnp.tanh(SCALE * pre * (1.0 + CUBIC * square))
        half = 0.5 + 0.5 * bend
        hidden[:, cols] = (pre * half).astype(jnp.bfloat16)
        slope[:, cols] = half + (0.5 * SCALE) * pre * (1.0 - bend * bend) * (
            1.0 + (3.0 * CUBIC) * square
        )

    down_copy.wait()

    def merge(kind, product, meanwhile):
        @pl.loop(0, width // CHUNK)
        def _(c):
            cols = pl.ds(pl.multiple_of(c * CHUNK, CHUNK), CHUNK)
            merge_send[kind, :, cols] = product(slots, cols).astype(jnp.bfloat16)

        swap = remote(
            merge_send.at[kind],
            merge_recv.at[kind],
            merge_ssem.at[kind],
            merge_rsem.at[kind],
            partner,
        )
        swap.start()

        @pl.loop(0, width // CHUNK)
        def _(c):
            cols = pl.ds(pl.multiple_of(c * CHUNK, CHUNK), CHUNK)
            mine[:, cols] = product(0, cols)

        meanwhile()
        swap.wait_recv()
        ret_send[kind] = (mine[...] + merge_recv[kind].astype(jnp.float32)).astype(jnp.bfloat16)
        send_all(2 + kind, ret_send.at[kind], ret_recv.at[kind])

    def out_product(start, cols):
        return jnp.dot(
            hidden[start : start + slots, :], down[:, cols], preferred_element_type=jnp.float32
        )

    merge(0, out_product, lambda: share(1, grad_send, grads, lambda k: None))

    shared(1, grads)
    across = (((1,), (1,)), ((), ()))

    @pl.loop(0, units // CHUNK)
    def _(c):
        cols = pl.ds(pl.multiple_of(c * CHUNK, CHUNK), CHUNK)
        dhid = lax.dot_general(
            grads[...], down[cols, :], across, preferred_element_type=jnp.float32
        )
        dpre[:, cols] = (dhid * slope[:, cols]).astype(jnp.bfloat16)

    def in_product(start, cols):
        return lax.dot_general(
            dpre[start : start + slots, :],
            up[cols, :],
            across,
            preferred_element_type=jnp.float32,
        )

    merge(1, in_product, lambda: None)

    rows_t[...] = rows[...].T

    @pl.loop(0, units // CHUNK)
    def _(c):
        cols = pl.ds(pl.multiple_of(c * CHUNK, CHUNK), CHUNK)
        ugrad_ref[0, :, cols] = jnp.dot(
            rows_t[...], dpre[:, cols], preferred_element_type=jnp.float32
        ).astype(jnp.bfloat16)
        dgrad_ref[0, cols, :] = lax.dot_general(
            hidden[:, cols],
            grads[...],
            (((0,), (0,)), ((), ())),
            preferred_element_type=jnp.float32,
        ).astype(jnp.bfloat16)

    def collect(kind):
        @pl.loop(1, n)
        def _(k):
            wait_block(2 + kind, ret_send.at[kind], ret_recv.at[kind], lax.rem(me + k, n))

        return jnp.dot(placing_t[...], ret_recv[kind], preferred_element_type=jnp.float32)

    returned = collect(0)
    out_ref[...] = (to_column(gate_ref[...]) * returned).astype(jnp.bfloat16)
    dots = jnp.sum(grad_ref[...].astype(jnp.float32) * returned, axis=1, keepdims=True)
    pgrad_ref[...] = jnp.sum(jnp.where(eye, dots, 0.0), axis=0, keepdims=True)
    tgrad_ref[...] = collect(1).astype(jnp.bfloat16)

    @pl.loop(1, n)
    def _(k):
        peer = lax.rem(me + k, n)
        exchange(0, tok_send, rows, peer, me).wait_send()
        exchange(1, grad_send, grads, peer, me).wait_send()
        exchange(2, ret_send.at[0], ret_recv.at[0], peer, me).wait_send()
        exchange(3, ret_send.at[1], ret_recv.at[1], peer, me).wait_send()

    @pl.loop(0, n)
    def _(k):
        forward(0, rows, k).wait_send()
        forward(1, grads, k).wait_send()

    for kind in range(2):
        remote(
            merge_send.at[kind],
            merge_recv.at[kind],
            merge_ssem.at[kind],
            merge_rsem.at[kind],
            partner,
        ).wait_send()


def local_fused(tokens, routing, gate_prob, up_weight, down_weight, out_grad):
    n = lax.axis_size("ep")
    count, width = tokens.shape
    units = up_weight.shape[2]
    cap = 2 * count // n
    slots = n * cap
    low, wide = jnp.bfloat16, jnp.float32
    vmem = pl.BlockSpec(memory_space=pltpu.VMEM)
    far = pl.BlockSpec(memory_space=pltpu.HBM)
    dma = pltpu.SemaphoreType.DMA
    output, token_grad, prob_grad, up_grad, down_grad = pl.pallas_call(
        functools.partial(kernel, n, cap),
        out_shape=(
            jax.ShapeDtypeStruct((count, width), low),
            jax.ShapeDtypeStruct((count, width), low),
            jax.ShapeDtypeStruct((1, count), wide),
            jax.ShapeDtypeStruct(up_weight.shape, low),
            jax.ShapeDtypeStruct(down_weight.shape, low),
        ),
        in_specs=[far] * 6,
        out_specs=(vmem,) * 5,
        scratch_shapes=[
            pltpu.VMEM((count, width), low),
            pltpu.VMEM((1, count), jnp.int32),
            pltpu.VMEM((1, count), wide),
            pltpu.VMEM((count, width), low),
            pltpu.VMEM((width, units), low),
            pltpu.VMEM((units, width), low),
            pltpu.VMEM((slots, width), low),
            pltpu.VMEM((slots, width), low),
            pltpu.VMEM((2 * slots, width), low),
            pltpu.VMEM((2 * slots, width), low),
            pltpu.VMEM((width, 2 * slots), low),
            pltpu.VMEM((2 * slots, units), low),
            pltpu.VMEM((2 * slots, units), wide),
            pltpu.VMEM((2 * slots, units), low),
            pltpu.VMEM((slots, width), wide),
            pltpu.VMEM((2, slots, width), low),
            pltpu.VMEM((2, slots, width), low),
            pltpu.VMEM((2, slots, width), low),
            pltpu.VMEM((2, slots, width), low),
            pltpu.VMEM((count, slots), low),
            dma((6,)),
            dma((4, n)),
            dma((4, n)),
            dma((2, n)),
            dma((2, n)),
            dma((2,)),
            dma((2,)),
        ],
        compiler_params=pltpu.CompilerParams(
            collective_id=0, has_side_effects=True, vmem_limit_bytes=48 << 20
        ),
        cost_estimate=pl.CostEstimate(
            flops=12 * 2 * slots * width * units,
            bytes_accessed=8 * width * units,
            transcendentals=2 * slots * units,
        ),
    )(
        tokens,
        routing.reshape(1, count),
        gate_prob.reshape(1, count),
        up_weight,
        down_weight,
        out_grad,
    )
    return (output, token_grad, prob_grad.reshape(count), up_grad, down_grad)


def local(tokens, routing, gate_prob, up_weight, down_weight, out_grad):
    n = lax.axis_size("ep")
    count, width = tokens.shape
    fits = (
        up_weight.shape[0] == 1
        and lax.axis_size("dp") == 2
        and (2 * count // n) % TILE == 0
        and (2 * count) % n == 0
        and up_weight.shape[2] % CHUNK == 0
        and width % CHUNK == 0
    )
    run = local_fused if fits else local_plain
    return run(tokens, routing, gate_prob, up_weight, down_weight, out_grad)


def solution(mesh):
    placed = (
        P(("ep", "dp"), None),
        P(("ep", "dp"), None),
        P(("ep", "dp")),
        P("ep", None, "dp"),
        P("ep", "dp", None),
        P(("ep", "dp"), None),
    )
    return jax.shard_map(
        local,
        mesh=mesh,
        in_specs=placed,
        out_specs=(
            P(("ep", "dp"), None),
            P(("ep", "dp"), None),
            P(("ep", "dp")),
            P("ep", None, "dp"),
            P("ep", "dp", None),
        ),
        check_vma=False,
    )
```

```python
import functools

import jax
import jax.numpy as jnp
from jax import lax
from jax.experimental import pallas as pl
from jax.experimental.pallas import tpu as pltpu
from jax.sharding import PartitionSpec as P


def local_plain(tokens, routing, gate_prob, up_weight, down_weight, out_grad):
    token_count = tokens.shape[0]
    local_experts = up_weight.shape[0]
    peer_count = lax.axis_size("ep")
    experts = local_experts * peer_count
    capacity = max(2, 2 * token_count // experts)
    slot_count = experts * capacity
    expert = routing[:, 0]
    onehot = (expert[:, None] == jnp.arange(experts, dtype=jnp.int32)[None, :]).astype(jnp.int32)
    ranking = jnp.sum((jnp.cumsum(onehot, axis=0) - onehot) * onehot, axis=1)
    target = expert * capacity + ranking
    placing = (jnp.arange(slot_count, dtype=jnp.int32)[:, None] == target[None, :]).astype(
        jnp.bfloat16
    )

    def dispatch(values):
        packed = jnp.dot(placing, values, preferred_element_type=jnp.float32).astype(jnp.bfloat16)
        return packed.reshape(experts, capacity, values.shape[1])

    def collect(returned):
        flat = returned.reshape(slot_count, returned.shape[2])
        return jnp.einsum("st,sd->td", placing, flat, preferred_element_type=jnp.float32)

    grad_wide = out_grad.astype(jnp.float32)
    scaled = (gate_prob[:, None] * grad_wide).astype(jnp.bfloat16)
    sent_rows = lax.all_to_all(dispatch(tokens), "ep", split_axis=0, concat_axis=1, tiled=True)
    expert_rows = lax.all_gather(sent_rows, "dp", axis=1, tiled=True)
    up_full, down_full = (up_weight, down_weight)
    preact = jnp.einsum("erd,edf->erf", expert_rows, up_full, preferred_element_type=jnp.float32)
    activated, back_fn = jax.vjp(jax.nn.gelu, preact)
    hidden = activated.astype(jnp.bfloat16)
    partial_out = jnp.einsum("erf,efd->erd", hidden, down_full, preferred_element_type=jnp.float32)
    merged = lax.psum_scatter(partial_out, "dp", scatter_dimension=1, tiled=True)
    expert_out = lax.all_to_all(
        merged.astype(jnp.bfloat16), "ep", split_axis=1, concat_axis=0, tiled=True
    )
    expert_tok = collect(expert_out)
    output = (gate_prob[:, None] * expert_tok).astype(jnp.bfloat16)
    prob_grad = jnp.sum(grad_wide * expert_tok, axis=1)
    sent_grads = lax.all_to_all(dispatch(scaled), "ep", split_axis=0, concat_axis=1, tiled=True)
    grad_rows = lax.all_gather(sent_grads, "dp", axis=1, tiled=True)
    hidden_grad = jnp.einsum(
        "erd,efd->erf", grad_rows, down_full, preferred_element_type=jnp.float32
    )
    preact_grad = back_fn(hidden_grad)[0].astype(jnp.bfloat16)
    partial_input = jnp.einsum(
        "erf,edf->erd", preact_grad, up_full, preferred_element_type=jnp.float32
    )
    up_sum = jnp.einsum(
        "erd,erf->edf", expert_rows, preact_grad, preferred_element_type=jnp.float32
    )
    down_sum = jnp.einsum("erf,erd->efd", hidden, grad_rows, preferred_element_type=jnp.float32)
    input_rows = lax.psum_scatter(partial_input, "dp", scatter_dimension=1, tiled=True)
    up_grad = up_sum.astype(jnp.bfloat16)
    down_grad = down_sum.astype(jnp.bfloat16)
    returned = lax.all_to_all(
        input_rows.astype(jnp.bfloat16), "ep", split_axis=1, concat_axis=0, tiled=True
    )
    token_grad = collect(returned).astype(jnp.bfloat16)
    return (output, token_grad, prob_grad, up_grad, down_grad)


MESH = pl.DeviceIdType.MESH
TILE = 16
CHUNK = 256
SCALE = 0.7978845608028654
CUBIC = 0.044715


def row_block(start, size):
    return pl.ds(pl.multiple_of(start, TILE), size)


def kernel(
    n,
    cap,
    tok_hbm,
    route_hbm,
    gate_hbm,
    up_hbm,
    down_hbm,
    grad_hbm,
    out_ref,
    tgrad_ref,
    pgrad_ref,
    ugrad_ref,
    dgrad_ref,
    tok_ref,
    route_ref,
    gate_ref,
    grad_ref,
    up,
    down,
    tok_send,
    grad_send,
    rows,
    grads,
    rows_t,
    hidden,
    slope,
    dpre,
    mine,
    merge_send,
    merge_recv,
    ret_send,
    ret_recv,
    placing_t,
    weight_sem,
    ep_send,
    ep_recv,
    dp_send,
    dp_recv,
    merge_ssem,
    merge_rsem,
):
    me, core = lax.axis_index("ep"), lax.axis_index("dp")
    partner = (me, 1 - core)
    slots = n * cap
    count, width = tok_ref.shape
    units = up.shape[1]

    staged = [
        pltpu.make_async_copy(far, near, weight_sem.at[2 + i])
        for i, (far, near) in enumerate(
            (
                (route_hbm, route_ref),
                (tok_hbm, tok_ref),
                (gate_hbm, gate_ref),
                (grad_hbm, grad_ref),
            )
        )
    ]
    for copy in staged:
        copy.start()
    barrier = pltpu.get_barrier_semaphore()

    @pl.loop(1, n)
    def _(k):
        pl.semaphore_signal(
            barrier, inc=1, device_id=(lax.rem(me + k, n), core), device_id_type=MESH
        )

    pl.semaphore_signal(barrier, inc=1, device_id=partner, device_id_type=MESH)
    up_copy = pltpu.make_async_copy(up_hbm.at[0], up, weight_sem.at[0])
    down_copy = pltpu.make_async_copy(down_hbm.at[0], down, weight_sem.at[1])
    up_copy.start()
    down_copy.start()

    def remote(src, dst, ssem, rsem, device):
        return pltpu.make_async_remote_copy(
            src_ref=src,
            dst_ref=dst,
            send_sem=ssem,
            recv_sem=rsem,
            device_id=device,
            device_id_type=MESH,
        )

    def exchange(kind, src, dst, peer, slot):
        return remote(
            src.at[row_block(peer * cap, cap)],
            dst.at[row_block(slot * cap, cap)],
            ep_send.at[kind, peer],
            ep_recv.at[kind, slot],
            (peer, core),
        )

    def send_all(kind, src, dst):
        @pl.loop(1, n)
        def _(k):
            exchange(kind, src, dst, lax.rem(me + k, n), me).start()

        dst[row_block(me * cap, cap), :] = src[row_block(me * cap, cap), :]

    def wait_block(kind, src, dst, source):
        exchange(kind, src, dst, source, source).wait_recv()

    def forward(kind, buf, source):
        return remote(
            buf.at[row_block(source * cap, cap)],
            buf.at[row_block(slots + source * cap, cap)],
            dp_send.at[kind, source],
            dp_recv.at[kind, source],
            partner,
        )

    def share(kind, src, dst, then):
        forward(kind, dst, me).start()

        @pl.loop(1, n)
        def _(k):
            source = lax.rem(me + n - k, n)
            wait_block(kind, src, dst, source)
            forward(kind, dst, source).start()
            then(k)

    def shared(kind, dst):
        @pl.loop(0, n)
        def _(k):
            forward(kind, dst, k).wait_recv()

    eye = lax.broadcasted_iota(jnp.int32, (count, count), 0) == lax.broadcasted_iota(
        jnp.int32, (count, count), 1
    )

    def to_column(row):
        return jnp.sum(jnp.where(eye, row, 0.0), axis=1, keepdims=True)

    staged[0].wait()
    expert = route_ref[...]
    onehot = (lax.broadcasted_iota(jnp.int32, (n, count), 0) == expert).astype(jnp.float32)
    before = (
        lax.broadcasted_iota(jnp.int32, (count, count), 0)
        < lax.broadcasted_iota(jnp.int32, (count, count), 1)
    ).astype(jnp.float32)
    earlier = jnp.dot(
        onehot.astype(jnp.bfloat16),
        before.astype(jnp.bfloat16),
        preferred_element_type=jnp.float32,
    )
    target = expert.astype(jnp.float32) * cap + jnp.sum(earlier * onehot, axis=0, keepdims=True)
    slot_rows = lax.broadcasted_iota(jnp.int32, (slots, count), 0).astype(jnp.float32)
    placing = (slot_rows == target).astype(jnp.float32).astype(jnp.bfloat16)
    staged[1].wait()
    tok_send[...] = jnp.dot(
        placing, tok_ref[...], preferred_element_type=jnp.float32
    ).astype(jnp.bfloat16)
    pl.semaphore_wait(barrier, n)
    send_all(0, tok_send, rows)

    staged[2].wait()
    staged[3].wait()
    gate = to_column(gate_ref[...])
    scaled = (gate * grad_ref[...].astype(jnp.float32)).astype(jnp.bfloat16)
    grad_send[...] = jnp.dot(
        placing, scaled, preferred_element_type=jnp.float32
    ).astype(jnp.bfloat16)
    grads[row_block(me * cap, cap), :] = grad_send[row_block(me * cap, cap), :]
    slot_cols = lax.broadcasted_iota(jnp.int32, (count, slots), 1).astype(jnp.float32)
    placing_t[...] = (slot_cols == to_column(target)).astype(jnp.float32).astype(jnp.bfloat16)

    def send_grads(k):
        exchange(1, grad_send, grads, lax.rem(me + k, n), me).start()

    share(0, tok_send, rows, send_grads)
    shared(0, rows)
    up_copy.wait()

    @pl.loop(0, units // CHUNK)
    def _(c):
        cols = pl.ds(pl.multiple_of(c * CHUNK, CHUNK), CHUNK)
        pre = jnp.dot(rows[...], up[:, cols], preferred_element_type=jnp.float32)
        square = pre * pre
        bend = jnp.tanh(SCALE * pre * (1.0 + CUBIC * square))
        half = 0.5 + 0.5 * bend
        hidden[:, cols] = (pre * half).astype(jnp.bfloat16)
        slope[:, cols] = half + (0.5 * SCALE) * pre * (1.0 - bend * bend) * (
            1.0 + (3.0 * CUBIC) * square
        )

    down_copy.wait()

    def merge(kind, product, meanwhile):
        @pl.loop(0, width // CHUNK)
        def _(c):
            cols = pl.ds(pl.multiple_of(c * CHUNK, CHUNK), CHUNK)
            merge_send[kind, :, cols] = product(slots, cols).astype(jnp.bfloat16)

        swap = remote(
            merge_send.at[kind],
            merge_recv.at[kind],
            merge_ssem.at[kind],
            merge_rsem.at[kind],
            partner,
        )
        swap.start()

        @pl.loop(0, width // CHUNK)
        def _(c):
            cols = pl.ds(pl.multiple_of(c * CHUNK, CHUNK), CHUNK)
            mine[:, cols] = product(0, cols)

        meanwhile()
        swap.wait_recv()
        ret_send[kind] = (mine[...] + merge_recv[kind].astype(jnp.float32)).astype(jnp.bfloat16)
        send_all(2 + kind, ret_send.at[kind], ret_recv.at[kind])

    def out_product(start, cols):
        return jnp.dot(
            hidden[start : start + slots, :], down[:, cols], preferred_element_type=jnp.float32
        )

    merge(0, out_product, lambda: share(1, grad_send, grads, lambda k: None))

    shared(1, grads)
    across = (((1,), (1,)), ((), ()))

    @pl.loop(0, units // CHUNK)
    def _(c):
        cols = pl.ds(pl.multiple_of(c * CHUNK, CHUNK), CHUNK)
        dhid = lax.dot_general(
            grads[...], down[cols, :], across, preferred_element_type=jnp.float32
        )
        dpre[:, cols] = (dhid * slope[:, cols]).astype(jnp.bfloat16)

    def in_product(start, cols):
        return lax.dot_general(
            dpre[start : start + slots, :],
            up[cols, :],
            across,
            preferred_element_type=jnp.float32,
        )

    merge(1, in_product, lambda: None)

    rows_t[...] = rows[...].T

    @pl.loop(0, units // CHUNK)
    def _(c):
        cols = pl.ds(pl.multiple_of(c * CHUNK, CHUNK), CHUNK)
        ugrad_ref[0, :, cols] = jnp.dot(
            rows_t[...], dpre[:, cols], preferred_element_type=jnp.float32
        ).astype(jnp.bfloat16)
        dgrad_ref[0, cols, :] = lax.dot_general(
            hidden[:, cols],
            grads[...],
            (((0,), (0,)), ((), ())),
            preferred_element_type=jnp.float32,
        ).astype(jnp.bfloat16)

    def collect(kind):
        @pl.loop(1, n)
        def _(k):
            wait_block(2 + kind, ret_send.at[kind], ret_recv.at[kind], lax.rem(me + k, n))

        return jnp.dot(placing_t[...], ret_recv[kind], preferred_element_type=jnp.float32)

    returned = collect(0)
    out_ref[...] = (to_column(gate_ref[...]) * returned).astype(jnp.bfloat16)
    dots = jnp.sum(grad_ref[...].astype(jnp.float32) * returned, axis=1, keepdims=True)
    pgrad_ref[...] = jnp.sum(jnp.where(eye, dots, 0.0), axis=0, keepdims=True)
    tgrad_ref[...] = collect(1).astype(jnp.bfloat16)

    @pl.loop(1, n)
    def _(k):
        peer = lax.rem(me + k, n)
        exchange(0, tok_send, rows, peer, me).wait_send()
        exchange(1, grad_send, grads, peer, me).wait_send()
        exchange(2, ret_send.at[0], ret_recv.at[0], peer, me).wait_send()
        exchange(3, ret_send.at[1], ret_recv.at[1], peer, me).wait_send()

    @pl.loop(0, n)
    def _(k):
        forward(0, rows, k).wait_send()
        forward(1, grads, k).wait_send()

    for kind in range(2):
        remote(
            merge_send.at[kind],
            merge_recv.at[kind],
            merge_ssem.at[kind],
            merge_rsem.at[kind],
            partner,
        ).wait_send()


def local_fused(tokens, routing, gate_prob, up_weight, down_weight, out_grad):
    n = lax.axis_size("ep")
    count, width = tokens.shape
    units = up_weight.shape[2]
    cap = 2 * count // n
    slots = n * cap
    low, wide = jnp.bfloat16, jnp.float32
    vmem = pl.BlockSpec(memory_space=pltpu.VMEM)
    far = pl.BlockSpec(memory_space=pltpu.HBM)
    dma = pltpu.SemaphoreType.DMA
    output, token_grad, prob_grad, up_grad, down_grad = pl.pallas_call(
        functools.partial(kernel, n, cap),
        out_shape=(
            jax.ShapeDtypeStruct((count, width), low),
            jax.ShapeDtypeStruct((count, width), low),
            jax.ShapeDtypeStruct((1, count), wide),
            jax.ShapeDtypeStruct(up_weight.shape, low),
            jax.ShapeDtypeStruct(down_weight.shape, low),
        ),
        in_specs=[far] * 6,
        out_specs=(vmem,) * 5,
        scratch_shapes=[
            pltpu.VMEM((count, width), low),
            pltpu.VMEM((1, count), jnp.int32),
            pltpu.VMEM((1, count), wide),
            pltpu.VMEM((count, width), low),
            pltpu.VMEM((width, units), low),
            pltpu.VMEM((units, width), low),
            pltpu.VMEM((slots, width), low),
            pltpu.VMEM((slots, width), low),
            pltpu.VMEM((2 * slots, width), low),
            pltpu.VMEM((2 * slots, width), low),
            pltpu.VMEM((width, 2 * slots), low),
            pltpu.VMEM((2 * slots, units), low),
            pltpu.VMEM((2 * slots, units), wide),
            pltpu.VMEM((2 * slots, units), low),
            pltpu.VMEM((slots, width), wide),
            pltpu.VMEM((2, slots, width), low),
            pltpu.VMEM((2, slots, width), low),
            pltpu.VMEM((2, slots, width), low),
            pltpu.VMEM((2, slots, width), low),
            pltpu.VMEM((count, slots), low),
            dma((6,)),
            dma((4, n)),
            dma((4, n)),
            dma((2, n)),
            dma((2, n)),
            dma((2,)),
            dma((2,)),
        ],
        compiler_params=pltpu.CompilerParams(
            collective_id=0, has_side_effects=True, vmem_limit_bytes=48 << 20
        ),
        cost_estimate=pl.CostEstimate(
            flops=12 * 2 * slots * width * units,
            bytes_accessed=8 * width * units,
            transcendentals=2 * slots * units,
        ),
    )(
        tokens,
        routing.reshape(1, count),
        gate_prob.reshape(1, count),
        up_weight,
        down_weight,
        out_grad,
    )
    return (output, token_grad, prob_grad.reshape(count), up_grad, down_grad)


def local(tokens, routing, gate_prob, up_weight, down_weight, out_grad):
    n = lax.axis_size("ep")
    count, width = tokens.shape
    fits = (
        up_weight.shape[0] == 1
        and lax.axis_size("dp") == 2
        and (2 * count // n) % TILE == 0
        and (2 * count) % n == 0
        and up_weight.shape[2] % CHUNK == 0
        and width % CHUNK == 0
    )
    run = local_fused if fits else local_plain
    return run(tokens, routing, gate_prob, up_weight, down_weight, out_grad)


def solution(mesh):
    placed = (
        P(("ep", "dp"), None),
        P(("ep", "dp"), None),
        P(("ep", "dp")),
        P("ep", None, "dp"),
        P("ep", "dp", None),
        P(("ep", "dp"), None),
    )
    return jax.shard_map(
        local,
        mesh=mesh,
        in_specs=placed,
        out_specs=(
            P(("ep", "dp"), None),
            P(("ep", "dp"), None),
            P(("ep", "dp")),
            P("ep", None, "dp"),
            P("ep", "dp", None),
        ),
        check_vma=False,
    )
```
